1024 devices in a mesh: aux: 16 (over z), row: 8 (over x, core), col: 8 (over y).
Axes of the slice: x: 4, y: 8, z: 16, core: 2. Of those that a mesh axis runs over, the one named last changes fastest.
Arguments:
- three_index: bfloat16 [10240, 3, 4608], P(('aux', 'row')), may hold values from -0.59765625 to 0.59765625
- vir_coef: bfloat16 [4608, 4096], P(None, 'col'), may hold values from -0.09375 to 0.09375
- owner_count: int32 [128], P(('aux', 'row')), may hold values from 20 to 80, as said below
- pair_index: int32 [2, 2], replicated, may hold values from 0 to 2, as said below
- occ_energy: float32 [3], replicated, may hold values from -2 to -0.6
- vir_energy: float32 [4096], replicated, may hold values from 0.3 to 3
Outputs:
- aux_density: float32 [10240, 2, 4096], P(('aux', 'row'), None, 'col')
The draws below stay inside these ranges and needn't reach their ends.
Inputs may be any that keep to these rules, and one draw needn't show every extreme that they name: `owner_count`: each owner holds between 20 and 80 live functions; both ends are reached in every draw. `pair_index`: i and j of a pair differ; every occupied orbital of the window appears.
All inputs are finite; a program needn't handle non-finite values.
Results may differ from the reference program's by a relative error of at most 0.022.
Values may be sent and summed in bfloat16 or wider, within the bound.
No kernel may reach another device: no remote copies, remote signals or barrier semaphores. Data moves between devices by JAX's collectives and lax.ppermute only.
A program may use at most 64 MiB of HBM per device.

```python
import jax
import jax.numpy as jnp

NVIR = 4096
NBAS = 4608
OCC_W = 3
PAIRS = 2
CAP = 80
OWNERS = 128
SLOTS = 10240


def draw_owner_count(key, part):
    lowest = CAP // 4
    counts = jax.random.randint(jax.random.fold_in(key, 11), (OWNERS,), lowest, CAP + 1)
    order = jax.random.permutation(jax.random.fold_in(key, 12), OWNERS)
    counts = counts.at[order[0]].set(CAP)
    counts = counts.at[order[1]].set(lowest)
    return counts.astype(jnp.int32)


def draw_pair_index(key, part):
    order = jax.random.permutation(jax.random.fold_in(key, 21), OCC_W)
    number = jnp.arange(PAIRS, dtype=jnp.int32)
    first_occ = jnp.take(order, number % OCC_W)
    second_occ = jnp.take(order, (number + 1) % OCC_W)
    return jnp.stack([first_occ, second_occ], axis=1).astype(jnp.int32)


def steps_of(key, extent, pieces, least, top_value):
    loudness, own = 1.0, jax.random.fold_in(key, 6)
    for dim, blocks in pieces:
        steps = jnp.exp(jax.random.uniform(jax.random.fold_in(own, dim), (blocks,), jnp.float32, least / len(pieces), top_value / len(pieces)))
        loudness = loudness * jnp.repeat(steps, extent[dim] // blocks).reshape([-1 if axis == dim else 1 for axis in range(len(extent))])
    return loudness


def normal_values(rng, extent, scale, reach, pieces=(), kind=jnp.bfloat16):
    values = scale * jax.random.normal(rng, extent, jnp.float32)
    if pieces:
        values = values * steps_of(rng, extent, pieces, -0.22, 0.18)
    return jnp.clip(values, -reach, reach).astype(kind)


def setup_inputs(seed: int = 0) -> dict:
    arg_keys = jax.random.split(jax.random.key(seed), 7)
    three_index = normal_values(arg_keys[0], (SLOTS, OCC_W, NBAS), 0.1, 0.59765625, ((0, 128),))
    vir_coef = normal_values(arg_keys[1], (NBAS, NVIR), NBAS ** -0.5, 0.09375, ((1, 8),))
    owner_count = draw_owner_count(jax.random.fold_in(arg_keys[6], 71), 0)
    pair_index = draw_pair_index(jax.random.fold_in(arg_keys[6], 71), 0)
    occ_energy = jnp.clip(jax.random.uniform(arg_keys[4], (OCC_W,), jnp.float32, -2.0, -0.6), -2.0, -0.6)
    vir_energy = jnp.clip(jax.random.uniform(arg_keys[5], (NVIR,), jnp.float32, 0.3, 3.0), 0.3, 3.0)
    return {"three_index": three_index, "vir_coef": vir_coef, "owner_count": owner_count, "pair_index": pair_index, "occ_energy": occ_energy, "vir_energy": vir_energy}


def reference(three_index, vir_coef, owner_count, pair_index, occ_energy, vir_energy):
    slot_total = three_index.shape[0]
    flat_rows = three_index.reshape(slot_total * OCC_W, NBAS)
    transformed = jnp.dot(flat_rows, vir_coef, preferred_element_type=jnp.float32).reshape(slot_total, OCC_W, NVIR)
    position = jnp.arange(slot_total, dtype=jnp.int32) % CAP
    owner_id = jnp.arange(slot_total, dtype=jnp.int32) // CAP
    is_live = position < jnp.take(owner_count, owner_id)
    bvec = jnp.where(is_live[:, None, None], transformed, jnp.zeros_like(transformed)).astype(jnp.bfloat16)
    results = []
    for pair_number in range(PAIRS):
        first_occ = pair_index[pair_number, 0]
        second_occ = pair_index[pair_number, 1]
        first_rows = jnp.take(bvec, first_occ, axis=1)
        second_rows = jnp.take(bvec, second_occ, axis=1)
        coulomb = jnp.dot(first_rows.T, second_rows, preferred_element_type=jnp.float32)
        pair_energy = jnp.take(occ_energy, first_occ) + jnp.take(occ_energy, second_occ)
        denominator = pair_energy - vir_energy[:, None] - vir_energy[None, :]
        amplitude = (coulomb / denominator).astype(jnp.bfloat16)
        results.append(jnp.dot(first_rows, amplitude, preferred_element_type=jnp.float32))
    return jnp.stack(results, axis=1)
```

```python
import jax
import jax.numpy as jnp
from jax import lax
from jax.experimental import pallas as pl
from jax.experimental.pallas import tpu as pltpu
from jax.sharding import Mesh, PartitionSpec as P

VMEM_LIMIT = 48 * 1024 * 1024
f32, bf16 = jnp.float32, jnp.bfloat16

NAMES = ("zh", "zl", "x", "k", "y")
S1, S2 = "x", "zh"
GM = "zl"


def params():
    return pltpu.CompilerParams(vmem_limit_bytes=VMEM_LIMIT)


def transform(rows, coef, count, pairs):
    occ, slots, basis = rows.shape
    width = coef.shape[1]
    pair_total = pairs.shape[0]
    step = 512
    steps = basis // step

    def kernel(count_ref, pairs_ref, rows_ref, coef_ref, first_ref, second_ref, total, held):
        at = pl.program_id(0)

        @pl.when(at == 0)
        def _():
            total[...] = jnp.zeros_like(total)

        total[...] += jnp.dot(
            rows_ref[...].reshape(occ * slots, step), coef_ref[...], preferred_element_type=f32
        )

        @pl.when(at == steps - 1)
        def _():
            value = total[...].reshape(occ, slots, width)
            place = lax.broadcasted_iota(jnp.int32, (occ, slots, width), 1)
            held[...] = jnp.where(place < count_ref[0], value, 0.0).astype(bf16)
            for q in range(pair_total):
                first_ref[q] = held[pairs_ref[q, 0]]
                second_ref[q] = held[pairs_ref[q, 1]]

    out = jax.ShapeDtypeStruct((pair_total, slots, width), bf16)
    whole = pl.BlockSpec((pair_total, slots, width), lambda i: (0, 0, 0))
    return pl.pallas_call(
        kernel,
        grid=(steps,),
        in_specs=[
            pl.BlockSpec(memory_space=pltpu.SMEM),
            pl.BlockSpec(memory_space=pltpu.SMEM),
            pl.BlockSpec((occ, slots, step), lambda i: (0, 0, i)),
            pl.BlockSpec((step, width), lambda i: (i, 0)),
        ],
        out_specs=[whole, whole],
        out_shape=[out, out],
        scratch_shapes=[
            pltpu.VMEM((occ * slots, width), f32),
            pltpu.VMEM((occ, slots, width), bf16),
        ],
        compiler_params=params(),
    )(count, pairs, rows, coef)


def coulomb_parts(first, second, n1, n2):
    owners, pair_total, slots, width = first.shape
    piece = width // (n1 * n2)

    def kernel(first_ref, second_ref, out_ref):
        a = first_ref[...].reshape(owners * slots, width)
        b = second_ref[...].reshape(owners * slots, width)
        value = lax.dot_general(a, b, (((0,), (0,)), ((), ())), preferred_element_type=f32)
        out_ref[...] = value.astype(bf16).reshape(n1, n2, 1, piece, width)

    block = pl.BlockSpec((owners, 1, slots, width), lambda q: (0, q, 0, 0))
    return pl.pallas_call(
        kernel,
        grid=(pair_total,),
        in_specs=[block, block],
        out_specs=pl.BlockSpec((n1, n2, 1, piece, width), lambda q: (0, 0, q, 0, 0)),
        out_shape=jax.ShapeDtypeStruct((n1, n2, pair_total, piece, width), bf16),
        compiler_params=params(),
    )(first, second)


def density_parts(first, amplitude, gm, cores):
    owners, pair_total, slots, width = first.shape
    n1, n2, _, piece, _ = amplitude.shape

    def kernel(first_ref, amp_ref, out_ref):
        a = first_ref[...].reshape(owners * slots, width)
        b = amp_ref[...].reshape(n1 * n2 * piece, width)
        value = jnp.dot(a, b, preferred_element_type=f32).astype(bf16)
        value = value.reshape(gm, cores, slots, width)
        for k in range(cores):
            for m in range(gm):
                out_ref[k, m, 0] = value[m, k]

    return pl.pallas_call(
        kernel,
        grid=(pair_total,),
        in_specs=[
            pl.BlockSpec((owners, 1, slots, width), lambda q: (0, q, 0, 0)),
            pl.BlockSpec((n1, n2, 1, piece, width), lambda q: (0, 0, q, 0, 0)),
        ],
        out_specs=pl.BlockSpec((cores, gm, 1, slots, width), lambda q: (0, 0, q, 0, 0)),
        out_shape=jax.ShapeDtypeStruct((cores, gm, pair_total, slots, width), bf16),
        compiler_params=params(),
    )(first, amplitude)


def added(parts):
    total = parts[0].astype(f32)
    for k in range(1, parts.shape[0]):
        total = total + parts[k].astype(f32)
    return total


def exchange(parts, axis):
    return lax.all_to_all(parts, axis, 0, 0, tiled=True)


def spread(part, axis):
    copies = jnp.broadcast_to(part[None], (lax.axis_size(axis),) + part.shape)
    return exchange(lax.optimization_barrier(copies), axis)


def make_local(sizes):
    gm, cores, cols = sizes[GM], sizes["k"], sizes["y"]
    n1, n2 = sizes[S1], sizes[S2]
    order = (GM, "k", "y")
    swap = []
    for m in range(gm):
        for k in range(cores):
            for y in range(cols):
                swap.append(((m * cores + k) * cols + y, y * cols + (m * cores + k)))

    def local(three_index, vir_coef, owner_count, pair_index, occ_energy, vir_energy):
        slots, occ, _ = three_index.shape
        width = vir_coef.shape[1]
        pair_total = pair_index.shape[0]
        rows = jnp.transpose(three_index, (1, 0, 2))
        first, second = transform(rows, vir_coef, owner_count, pair_index)
        second_all = lax.all_gather(second, (GM, "k"), axis=0, tiled=False)
        second_all = second_all.reshape((gm * cores,) + second.shape)
        first_turned = lax.ppermute(first, order, swap)
        first_all = spread(first_turned, "y")
        parts = coulomb_parts(first_all, second_all, n1, n2)
        mine = added(exchange(parts, S1)).astype(bf16)
        share = added(exchange(mine, S2))
        piece = width // (n1 * n2)
        block = lax.axis_index(GM) * cores + lax.axis_index("k")
        start = block * width + lax.axis_index(S1) * (width // n1) + lax.axis_index(S2) * piece
        first_vir = lax.dynamic_slice_in_dim(vir_energy, start, piece)
        second_vir = lax.dynamic_slice_in_dim(vir_energy, lax.axis_index("y") * width, width)
        mask = pair_index[:, :, None] == jnp.arange(occ, dtype=jnp.int32)
        pair_energy = jnp.sum(jnp.where(mask, occ_energy, 0.0), axis=(1, 2))
        denominator = pair_energy[:, None, None] - first_vir[:, None] - second_vir
        amp = (share / denominator).astype(bf16)
        amp_all = spread(spread(amp, S2), S1)
        dens = density_parts(first_all, amp_all, gm, cores)
        dens = added(exchange(dens, "k")).astype(bf16)
        out = added(exchange(dens, GM))
        return jnp.transpose(out, (1, 0, 2))

    return local


def solution(mesh):
    aux, row, col = (mesh.shape[name] for name in ("aux", "row", "col"))
    sizes = {"zl": 4, "zh": aux // 4, "k": 2, "x": row // 2, "y": col}
    fine = Mesh(mesh.devices.reshape([sizes[name] for name in NAMES]), NAMES)
    owners = ("zh", "zl", "x", "k")
    return jax.shard_map(
        make_local(sizes),
        mesh=fine,
        in_specs=(P(owners, None, None), P(None, "y"), P(owners), P(), P(), P()),
        out_specs=P(owners, None, "y"),
        check_vma=False,
    )
```

```python
import jax
import jax.numpy as jnp
from jax import lax
from jax.experimental import pallas as pl
from jax.experimental.pallas import tpu as pltpu
from jax.sharding import Mesh, PartitionSpec as P

VMEM_LIMIT = 48 * 1024 * 1024
f32, bf16 = jnp.float32, jnp.bfloat16

NAMES = ("zh", "zl", "x", "k", "y")
S1, S2 = "x", "zh"
GM = "zl"


def params():
    return pltpu.CompilerParams(vmem_limit_bytes=VMEM_LIMIT)


def transform(rows, coef, count, pairs):
    occ, slots, basis = rows.shape
    width = coef.shape[1]
    pair_total = pairs.shape[0]
    step = 512
    steps = basis // step

    def kernel(count_ref, pairs_ref, rows_ref, coef_ref, first_ref, second_ref, coefs, held, sems):
        copies = [
            pltpu.make_async_copy(coef_ref.at[pl.ds(k * step, step)], coefs.at[k], sems.at[k])
            for k in range(steps)
        ]
        for copy in copies:
            copy.start()
        total = jnp.zeros((occ * slots, width), f32)
        for k in range(steps):
            copies[k].wait()
            part = rows_ref[:, :, k * step : (k + 1) * step].reshape(occ * slots, step)
            total += jnp.dot(part, coefs[k], preferred_element_type=f32)
        value = total.reshape(occ, slots, width)
        place = lax.broadcasted_iota(jnp.int32, (occ, slots, width), 1)
        held[...] = jnp.where(place < count_ref[0], value, 0.0).astype(bf16)
        for q in range(pair_total):
            first_ref[q] = held[pairs_ref[q, 0]]
            second_ref[q] = held[pairs_ref[q, 1]]

    out = jax.ShapeDtypeStruct((pair_total, slots, width), bf16)
    smem = pl.BlockSpec(memory_space=pltpu.SMEM)
    vmem = pl.BlockSpec(memory_space=pltpu.VMEM)
    return pl.pallas_call(
        kernel,
        in_specs=[smem, smem, vmem, pl.BlockSpec(memory_space=pl.ANY)],
        out_specs=[vmem, vmem],
        out_shape=[out, out],
        scratch_shapes=[
            pltpu.VMEM((steps, step, width), bf16),
            pltpu.VMEM((occ, slots, width), bf16),
            pltpu.SemaphoreType.DMA((steps,)),
        ],
        compiler_params=params(),
    )(count, pairs, rows, coef)


def coulomb_parts(first, second, n1, n2):
    groups, cores, pair_total, slots, width = first.shape
    piece = width // (n1 * n2)
    depth = groups * slots

    def kernel(first_ref, *refs):
        out_ref = refs[-1]
        value = jnp.zeros((width, width), f32)
        for k in range(cores):
            a = first_ref[:, k, 0].reshape(depth, width)
            b = refs[k][...].reshape(depth, width)
            value += lax.dot_general(a, b, (((0,), (0,)), ((), ())), preferred_element_type=f32)
        out_ref[...] = value.astype(bf16).reshape(n1, n2, 1, piece, width)

    return pl.pallas_call(
        kernel,
        grid=(pair_total,),
        in_specs=[pl.BlockSpec((groups, cores, 1, slots, width), lambda q: (0, 0, q, 0, 0))]
        + [pl.BlockSpec((groups, 1, slots, width), lambda q: (0, q, 0, 0))] * cores,
        out_specs=pl.BlockSpec((n1, n2, 1, piece, width), lambda q: (0, 0, q, 0, 0)),
        out_shape=jax.ShapeDtypeStruct((n1, n2, pair_total, piece, width), bf16),
        compiler_params=params(),
    )(first, *second)


def density_parts(first, amplitude, targets):
    groups, cores, pair_total, slots, width = first.shape
    n1, n2, _, piece, _ = amplitude.shape

    def kernel(targets_ref, first_ref, amp_ref, *outs):
        b = amp_ref[...].reshape(n1 * n2 * piece, width)
        for k in range(cores):
            a = first_ref[:, k, 0].reshape(groups * slots, width)
            value = jnp.dot(a, b, preferred_element_type=f32).astype(bf16)
            value = value.reshape(groups, slots, width)
            for m in range(groups):
                outs[k][targets_ref[m], 0] = value[m]

    return pl.pallas_call(
        kernel,
        grid=(pair_total,),
        in_specs=[
            pl.BlockSpec(memory_space=pltpu.SMEM),
            pl.BlockSpec((groups, cores, 1, slots, width), lambda q: (0, 0, q, 0, 0)),
            pl.BlockSpec((n1, n2, 1, piece, width), lambda q: (0, 0, q, 0, 0)),
        ],
        out_specs=[pl.BlockSpec((groups, 1, slots, width), lambda q: (0, q, 0, 0))] * cores,
        out_shape=[jax.ShapeDtypeStruct((groups, pair_total, slots, width), bf16)] * cores,
        compiler_params=params(),
    )(targets, first, amplitude)


def added(parts):
    total = parts[0].astype(f32)
    for k in range(1, parts.shape[0]):
        total = total + parts[k].astype(f32)
    return total


def exchange(parts, axis):
    return lax.all_to_all(parts, axis, 0, 0, tiled=True)


def spread(part, axis):
    copies = jnp.broadcast_to(part[None], (lax.axis_size(axis),) + part.shape)
    return exchange(lax.optimization_barrier(copies), axis)


def make_local(sizes):
    gm, cores, cols = sizes[GM], sizes["k"], sizes["y"]
    n1, n2 = sizes[S1], sizes[S2]
    order = (GM, "k", "y")
    turn = []
    for m in range(gm):
        for k in range(cores):
            for y in range(cols):
                to_m, to_k = y % gm, y // gm
                to_y = (to_m - m) % gm * cores + (k ^ to_k)
                turn.append(((m * cores + k) * cols + y, (to_m * cores + to_k) * cols + to_y))
    swap = [(0, 1), (1, 0)]

    def local(three_index, vir_coef, owner_count, pair_index, occ_energy, vir_energy):
        slots, occ, _ = three_index.shape
        width = vir_coef.shape[1]
        pair_total = pair_index.shape[0]
        rows = jnp.transpose(three_index, (1, 0, 2))
        first, second = transform(rows, vir_coef, owner_count, pair_index)
        turned = lax.ppermute(first, order, turn)
        piece = width // (n1 * n2)
        block = lax.axis_index("k") * gm + lax.axis_index(GM)
        start = block * width + lax.axis_index(S1) * (width // n1) + lax.axis_index(S2) * piece
        first_vir = lax.dynamic_slice_in_dim(vir_energy, start, piece)
        second_vir = lax.dynamic_slice_in_dim(vir_energy, lax.axis_index("y") * width, width)
        mask = pair_index[:, :, None] == jnp.arange(occ, dtype=jnp.int32)
        pair_energy = jnp.sum(jnp.where(mask, occ_energy, 0.0), axis=(1, 2))
        denominator = pair_energy[:, None, None] - first_vir[:, None] - second_vir
        targets = (lax.axis_index(GM) - jnp.arange(gm, dtype=jnp.int32)) % gm
        turned, denominator, targets = lax.optimization_barrier((turned, denominator, targets))
        copies = jnp.broadcast_to(turned[None], (cols,) + turned.shape)
        copies, second = lax.optimization_barrier((copies, second))
        first_all = exchange(copies, "y").reshape((gm, cores) + first.shape)
        rings = [second]
        for d in range(1, gm):
            rings.append(lax.ppermute(second, GM, [(m, (m + d) % gm) for m in range(gm)]))
        second_own = jnp.stack(rings)
        second_other = lax.ppermute(second_own, "k", swap)
        parts = coulomb_parts(first_all, (second_own, second_other), n1, n2)
        mine = added(exchange(parts, S1)).astype(bf16)
        share = added(exchange(mine, S2))
        amp = (share / denominator).astype(bf16)
        amp_all = spread(spread(amp, S2), S1)
        own, other = density_parts(first_all, amp_all, targets)
        came = lax.ppermute(other, "k", swap)
        dens = (own.astype(f32) + came.astype(f32)).astype(bf16)
        out = added(exchange(dens, GM))
        return jnp.transpose(out, (1, 0, 2))

    return local


def solution(mesh):
    aux, row, col = (mesh.shape[name] for name in ("aux", "row", "col"))
    sizes = {"zl": 4, "zh": aux // 4, "k": 2, "x": row // 2, "y": col}
    fine = Mesh(mesh.devices.reshape([sizes[name] for name in NAMES]), NAMES)
    owners = ("zh", "zl", "x", "k")
    return jax.shard_map(
        make_local(sizes),
        mesh=fine,
        in_specs=(P(owners, None, None), P(None, "y"), P(owners), P(), P(), P()),
        out_specs=P(owners, None, "y"),
        check_vma=False,
    )
```

```python
import jax
import jax.numpy as jnp
from jax import lax
from jax.experimental import pallas as pl
from jax.experimental.pallas import tpu as pltpu
from jax.sharding import Mesh, PartitionSpec as P

VMEM_LIMIT = 48 * 1024 * 1024
WIDE_LIMIT = 63 * 1024 * 1024
f32, bf16 = jnp.float32, jnp.bfloat16

NAMES = ("zh", "zl", "x", "k", "yh", "yl")
S1, S2 = "x", "zh"
GM = "zl"


def params():
    return pltpu.CompilerParams(vmem_limit_bytes=VMEM_LIMIT)


def transform(rows, coef, count, pairs, energies, place_of):
    occ, slots, basis = rows.shape
    width = coef.shape[1]
    step = 512
    steps = basis // step

    def kernel(
        count_hbm, pairs_hbm, energies_hbm, rows_hbm, coef_hbm,
        turn_a, turn_b, kept, given, energy,
        count_ref, pairs_ref, energies_ref, parts, coefs, held, sems, small,
    ):
        scalars = [
            pltpu.make_async_copy(count_hbm, count_ref, small.at[0]),
            pltpu.make_async_copy(pairs_hbm, pairs_ref, small.at[1]),
            pltpu.make_async_copy(energies_hbm, energies_ref, small.at[2]),
        ]
        copies = []
        for k in range(steps):
            span = pl.ds(k * step, step)
            copies.append(
                (
                    pltpu.make_async_copy(rows_hbm.at[:, :, span], parts.at[k], sems.at[0, k]),
                    pltpu.make_async_copy(coef_hbm.at[span], coefs.at[k], sems.at[1, k]),
                )
            )
        for pair in copies:
            for copy in pair:
                copy.start()
        for copy in scalars:
            copy.start()
        total = jnp.zeros((occ * slots, width), f32)
        for k in range(steps):
            for copy in copies[k]:
                copy.wait()
            part = parts[k].reshape(occ * slots, step)
            total += jnp.dot(part, coefs[k], preferred_element_type=f32)
        for copy in scalars:
            copy.wait()
        value = total.reshape(occ, slots, width)
        place = lax.broadcasted_iota(jnp.int32, (occ, slots, width), 1)
        held[...] = jnp.where(place < count_ref[0], value, 0.0).astype(bf16)
        half, core = place_of()
        turn_a[...] = held[pairs_ref[half, 0]]
        turn_b[...] = held[pairs_ref[1 - half, 0]]
        kept[...] = held[pairs_ref[core, 1]]
        given[...] = held[pairs_ref[1 - core, 1]]
        energy[0] = energies_ref[pairs_ref[core, 0]] + energies_ref[pairs_ref[core, 1]]

    out = jax.ShapeDtypeStruct((slots, width), bf16)
    hbm = pl.BlockSpec(memory_space=pl.ANY)
    vmem = pl.BlockSpec(memory_space=pltpu.VMEM)
    return pl.pallas_call(
        kernel,
        in_specs=[hbm] * 5,
        out_specs=[vmem] * 4 + [pl.BlockSpec(memory_space=pltpu.SMEM)],
        out_shape=[out] * 4 + [jax.ShapeDtypeStruct((1,), f32)],
        scratch_shapes=[
            pltpu.SMEM(count.shape, jnp.int32),
            pltpu.SMEM(pairs.shape, jnp.int32),
            pltpu.SMEM(energies.shape, f32),
            pltpu.VMEM((steps, occ, slots, step), bf16),
            pltpu.VMEM((steps, step, width), bf16),
            pltpu.VMEM((occ, slots, width), bf16),
            pltpu.SemaphoreType.DMA((2, steps)),
            pltpu.SemaphoreType.DMA((3,)),
        ],
        compiler_params=pltpu.CompilerParams(vmem_limit_bytes=WIDE_LIMIT),
    )(count, pairs, energies, rows, coef)


def flat(ref):
    return ref[...].reshape(-1, ref.shape[-1])


def coulomb_parts(side, first, second, n1, n2):
    groups, halves, slots, width = first[0].shape
    piece = width // (n1 * n2)

    def kernel(side_ref, near, low, high, *refs):
        out_ref = refs[-1]
        value = jnp.zeros((width, width), f32)
        held = [flat(near), jnp.concatenate([flat(low), flat(high)], axis=0)]
        for k in range(2):
            at = side_ref[0] if k == 0 else 1 - side_ref[0]
            b = jnp.concatenate([r[:, at].reshape(-1, width) for r in refs[:-1]], axis=0)
            value += lax.dot_general(
                held[k], b, (((0,), (0,)), ((), ())), preferred_element_type=f32
            )
        out_ref[...] = value.astype(bf16).reshape(n1, n2, 1, piece, width)

    return pl.pallas_call(
        kernel,
        grid=(halves,),
        in_specs=[pl.BlockSpec(memory_space=pltpu.SMEM)]
        + [pl.BlockSpec((f.shape[0], 1, slots, width), lambda h: (0, h, 0, 0)) for f in first]
        + [pl.BlockSpec(r.shape, lambda h: (0, 0, 0, 0)) for r in second],
        out_specs=pl.BlockSpec((n1, n2, 1, piece, width), lambda h: (0, 0, h, 0, 0)),
        out_shape=jax.ShapeDtypeStruct((n1, n2, halves, piece, width), bf16),
        compiler_params=params(),
    )(side, *first, *second)


def density_parts(side, targets, first, amplitude):
    groups, halves, slots, width = first[0].shape
    n1, n2, _, piece, _ = amplitude.shape

    def kernel(side_ref, targets_ref, near, low, high, amp_ref, out_ref):
        amps = [amp_ref[:, :, h].reshape(n1 * n2 * piece, width) for h in range(halves)]
        for k, refs in enumerate(((near,), (low, high))):
            value = 0.0
            for h in range(halves):
                a = jnp.concatenate([r[:, h].reshape(-1, width) for r in refs], axis=0)
                value += jnp.dot(a, amps[h], preferred_element_type=f32)
            value = value.astype(bf16).reshape(groups, slots, width)
            at = side_ref[0] if k == 0 else 1 - side_ref[0]
            for m in range(groups):
                out_ref[targets_ref[m], at] = value[m]

    smem = pl.BlockSpec(memory_space=pltpu.SMEM)
    vmem = pl.BlockSpec(memory_space=pltpu.VMEM)
    return pl.pallas_call(
        kernel,
        in_specs=[smem, smem] + [vmem] * 4,
        out_specs=vmem,
        out_shape=jax.ShapeDtypeStruct((groups, 2, slots, width), bf16),
        compiler_params=params(),
    )(side, targets, *first, amplitude)


def added(parts):
    total = parts[0].astype(f32)
    for k in range(1, parts.shape[0]):
        total = total + parts[k].astype(f32)
    return total


def exchange(parts, axis):
    return lax.all_to_all(parts, axis, 0, 0, tiled=True)


def spread(part, axis):
    copies = jnp.broadcast_to(part[None], (lax.axis_size(axis),) + part.shape)
    return exchange(lax.optimization_barrier(copies), axis)


def make_local(sizes):
    gm, cores, high, low = sizes[GM], sizes["k"], sizes["yh"], sizes["yl"]
    n1, n2 = sizes[S1], sizes[S2]
    cols = high * low
    order = (GM, "k", "yh", "yl")
    step = (0, 2, 1, 3)
    turns = [[], []]
    for m in range(gm):
        for k in range(cores):
            for y in range(cols):
                to_m, half = y % gm, y // gm
                to_y = step[to_m ^ m] * low + k
                for t in range(2):
                    to = (to_m * cores + (half ^ t)) * cols + to_y
                    turns[t].append(((m * cores + k) * cols + y, to))
    swap = [(0, 1), (1, 0)]
    up = [(y, (y + 1) % cols) for y in range(cols)]
    down = [(y, (y - 1) % cols) for y in range(cols)]
    across = [(m, m ^ 2) for m in range(gm)]
    beside = [(m, m ^ 1) for m in range(gm)]

    def column():
        return lax.axis_index("yh") * low + lax.axis_index("yl")

    def local(three_index, vir_coef, owner_count, pair_index, occ_energy, vir_energy):
        width = vir_coef.shape[1]
        core, group, side = lax.axis_index("k"), lax.axis_index(GM), lax.axis_index("yl")
        rows = jnp.transpose(three_index, (1, 0, 2))
        turn_a, turn_b, kept, given, energy = transform(
            rows, vir_coef, owner_count, pair_index, occ_energy,
            lambda: (column() // gm, lax.axis_index("k")),
        )
        turned = jnp.stack(
            [lax.ppermute(turn_a, order, turns[0]), lax.ppermute(turn_b, order, turns[1])]
        )

        piece = width // (n1 * n2)
        offset = lax.axis_index(S1) * (width // n1) + lax.axis_index(S2) * piece
        first_vir = jnp.stack(
            [
                lax.dynamic_slice_in_dim(vir_energy, (h * gm + group) * width + offset, piece)
                for h in (core, 1 - core)
            ]
        )
        second_vir = lax.dynamic_slice_in_dim(vir_energy, column() * width, width)
        denominator = energy[0] - first_vir[:, :, None] - second_vir
        targets = group ^ jnp.array(step, jnp.int32)
        flip = (side ^ core).astype(jnp.int32).reshape(1)
        second = jnp.stack([kept, lax.ppermute(given, "k", swap)])
        turned, second, denominator, targets, flip = lax.optimization_barrier(
            (turned, second, denominator, targets, flip)
        )

        near = spread(turned, "yh")
        second_held = jnp.stack([second, lax.ppermute(second, GM, across)])
        near, second_held = lax.optimization_barrier((near, second_held))
        second_beside = lax.ppermute(second_held, GM, beside)
        middle = high // 2
        far_low = lax.ppermute(near[:middle], ("yh", "yl"), up)
        far_high = lax.ppermute(near[middle:], ("yh", "yl"), down)
        first_all = [near, far_low, far_high]

        parts = coulomb_parts(flip, first_all, [second_held, second_beside], n1, n2)
        mine = added(exchange(parts, S1)).astype(bf16)
        share = added(exchange(mine, S2))
        amp = (share / denominator).astype(bf16)
        amp_all = spread(spread(amp, S2), S1)
        dens = added(exchange(density_parts(flip, targets, first_all, amp_all), GM))
        came = lax.ppermute(dens[1], "k", swap)
        out = [jnp.where(core == q, dens[0], came) for q in range(2)]
        return jnp.stack(out, axis=1)

    return local


def solution(mesh):
    aux, row, col = (mesh.shape[name] for name in ("aux", "row", "col"))
    sizes = {"zl": 4, "zh": aux // 4, "k": 2, "x": row // 2, "yh": col // 2, "yl": 2}
    fine = Mesh(mesh.devices.reshape([sizes[name] for name in NAMES]), NAMES)
    owners = ("zh", "zl", "x", "k")
    return jax.shard_map(
        make_local(sizes),
        mesh=fine,
        in_specs=(P(owners, None, None), P(None, ("yh", "yl")), P(owners), P(), P(), P()),
        out_specs=P(owners, None, ("yh", "yl")),
        check_vma=False,
    )
```

```python
import jax
import jax.numpy as jnp
from jax import lax
from jax.experimental import pallas as pl
from jax.experimental.pallas import tpu as pltpu
from jax.sharding import Mesh, PartitionSpec as P

VMEM_LIMIT = 48 * 1024 * 1024
WIDE_LIMIT = 63 * 1024 * 1024
f32, bf16 = jnp.float32, jnp.bfloat16

NAMES = ("zh", "zl", "x", "k", "yh", "yl")
S1, S2 = "x", "zh"
GM = "zl"


def params():
    return pltpu.CompilerParams(vmem_limit_bytes=VMEM_LIMIT)


def transform(rows, coef, count, pairs, energies, place_of):
    occ, slots, basis = rows.shape
    width = coef.shape[1]
    step = 512
    steps = basis // step

    def kernel(
        count_hbm, pairs_hbm, energies_hbm, rows_hbm, coef_hbm,
        turn_a, turn_b, kept, given, energy,
        count_ref, pairs_ref, energies_ref, parts, coefs, held, sems, small,
    ):
        scalars = [
            pltpu.make_async_copy(count_hbm, count_ref, small.at[0]),
            pltpu.make_async_copy(pairs_hbm, pairs_ref, small.at[1]),
            pltpu.make_async_copy(energies_hbm, energies_ref, small.at[2]),
        ]
        copies = []
        for k in range(steps):
            span = pl.ds(k * step, step)
            copies.append(
                (
                    pltpu.make_async_copy(rows_hbm.at[:, :, span], parts.at[k], sems.at[0, k]),
                    pltpu.make_async_copy(coef_hbm.at[span], coefs.at[k], sems.at[1, k]),
                )
            )
        for pair in copies:
            for copy in pair:
                copy.start()
        for copy in scalars:
            copy.start()
        total = jnp.zeros((occ * slots, width), f32)
        for k in range(steps):
            for copy in copies[k]:
                copy.wait()
            part = parts[k].reshape(occ * slots, step)
            total += jnp.dot(part, coefs[k], preferred_element_type=f32)
        for copy in scalars:
            copy.wait()
        value = total.reshape(occ, slots, width)
        place = lax.broadcasted_iota(jnp.int32, (occ, slots, width), 1)
        held[...] = jnp.where(place < count_ref[0], value, 0.0).astype(bf16)
        half, core = place_of()
        turn_a[...] = held[pairs_ref[half, 0]]
        turn_b[...] = held[pairs_ref[1 - half, 0]]
        kept[...] = held[pairs_ref[core, 1]]
        given[...] = held[pairs_ref[1 - core, 1]]
        energy[0] = energies_ref[pairs_ref[core, 0]] + energies_ref[pairs_ref[core, 1]]

    out = jax.ShapeDtypeStruct((slots, width), bf16)
    hbm = pl.BlockSpec(memory_space=pl.ANY)
    vmem = pl.BlockSpec(memory_space=pltpu.VMEM)
    return pl.pallas_call(
        kernel,
        in_specs=[hbm] * 5,
        out_specs=[vmem] * 4 + [pl.BlockSpec(memory_space=pltpu.SMEM)],
        out_shape=[out] * 4 + [jax.ShapeDtypeStruct((1,), f32)],
        scratch_shapes=[
            pltpu.SMEM(count.shape, jnp.int32),
            pltpu.SMEM(pairs.shape, jnp.int32),
            pltpu.SMEM(energies.shape, f32),
            pltpu.VMEM((steps, occ, slots, step), bf16),
            pltpu.VMEM((steps, step, width), bf16),
            pltpu.VMEM((occ, slots, width), bf16),
            pltpu.SemaphoreType.DMA((2, steps)),
            pltpu.SemaphoreType.DMA((3,)),
        ],
        compiler_params=pltpu.CompilerParams(vmem_limit_bytes=WIDE_LIMIT),
    )(count, pairs, energies, rows, coef)


def flat(ref):
    return ref[...].reshape(-1, ref.shape[-1])


def coulomb_parts(side, first, second, n1, n2):
    groups, halves, slots, width = first[0].shape
    piece = width // (n1 * n2)

    def kernel(side_ref, near, low, high, *refs):
        out_ref = refs[-1]
        value = jnp.zeros((width, width), f32)
        held = [flat(near), jnp.concatenate([flat(low), flat(high)], axis=0)]
        for k in range(2):
            at = side_ref[0] if k == 0 else 1 - side_ref[0]
            b = jnp.concatenate([r[at] for r in refs[:-1]], axis=0)
            value += lax.dot_general(
                held[k], b, (((0,), (0,)), ((), ())), preferred_element_type=f32
            )
        out_ref[...] = value.astype(bf16).reshape(n1, n2, 1, piece, width)

    return pl.pallas_call(
        kernel,
        grid=(halves,),
        in_specs=[pl.BlockSpec(memory_space=pltpu.SMEM)]
        + [pl.BlockSpec((f.shape[0], 1, slots, width), lambda h: (0, h, 0, 0)) for f in first]
        + [pl.BlockSpec(r.shape, lambda h: (0, 0, 0)) for r in second],
        out_specs=pl.BlockSpec((n1, n2, 1, piece, width), lambda h: (0, 0, h, 0, 0)),
        out_shape=jax.ShapeDtypeStruct((n1, n2, halves, piece, width), bf16),
        compiler_params=params(),
    )(side, *first, *second)


def density_parts(side, targets, first, amplitude):
    groups, halves, slots, width = first[0].shape
    n1, n2, _, piece, _ = amplitude.shape

    def kernel(side_ref, targets_ref, near, low, high, amp_ref, out_ref):
        amps = [amp_ref[:, :, h].reshape(n1 * n2 * piece, width) for h in range(halves)]
        for k, refs in enumerate(((near,), (low, high))):
            value = 0.0
            for h in range(halves):
                a = jnp.concatenate([r[:, h].reshape(-1, width) for r in refs], axis=0)
                value += jnp.dot(a, amps[h], preferred_element_type=f32)
            value = value.astype(bf16).reshape(groups, slots, width)
            at = side_ref[0] if k == 0 else 1 - side_ref[0]
            for m in range(groups):
                out_ref[targets_ref[m], at] = value[m]

    smem = pl.BlockSpec(memory_space=pltpu.SMEM)
    vmem = pl.BlockSpec(memory_space=pltpu.VMEM)
    return pl.pallas_call(
        kernel,
        in_specs=[smem, smem] + [vmem] * 4,
        out_specs=vmem,
        out_shape=jax.ShapeDtypeStruct((groups, 2, slots, width), bf16),
        compiler_params=params(),
    )(side, targets, *first, amplitude)


def added(parts):
    total = parts[0].astype(f32)
    for k in range(1, parts.shape[0]):
        total = total + parts[k].astype(f32)
    return total


def finish(core, parts, came):
    groups, members, slots, width = parts.shape

    def kernel(core_ref, parts_ref, came_ref, out_ref):
        total = parts_ref[0, 0].astype(f32)
        for m in range(1, groups):
            total += parts_ref[m, 0].astype(f32)
        came = came_ref[...]
        own = core_ref[0] == 0
        out_ref[:, 0, :] = jnp.where(own, total, came)
        out_ref[:, 1, :] = jnp.where(own, came, total)

    vmem = pl.BlockSpec(memory_space=pltpu.VMEM)
    return pl.pallas_call(
        kernel,
        grid=(1,),
        in_specs=[
            pl.BlockSpec(memory_space=pltpu.SMEM),
            pl.BlockSpec((groups, 1, slots, width), lambda i: (0, 0, 0, 0)),
            pl.BlockSpec((slots, width), lambda i: (0, 0)),
        ],
        out_specs=pl.BlockSpec((slots, 2, width), lambda i: (0, 0, 0)),
        out_shape=jax.ShapeDtypeStruct((slots, 2, width), f32),
        compiler_params=params(),
    )(core.astype(jnp.int32).reshape(1), parts, came)


def exchange(parts, axis):
    return lax.all_to_all(parts, axis, 0, 0, tiled=True)


def copied(parts, count):
    def kernel(*refs):
        for n in range(count):
            for i, part in enumerate(refs[:-1]):
                refs[-1][n, i] = part[...]

    vmem = pl.BlockSpec(memory_space=pltpu.VMEM)
    shape = (count, len(parts)) + parts[0].shape
    return pl.pallas_call(
        kernel,
        in_specs=[vmem] * len(parts),
        out_specs=vmem,
        out_shape=jax.ShapeDtypeStruct(shape, parts[0].dtype),
        compiler_params=params(),
    )(*parts)


def spread(part, axis):
    copies = jnp.broadcast_to(part[None], (lax.axis_size(axis),) + part.shape)
    return exchange(lax.optimization_barrier(copies), axis)


def make_local(sizes):
    gm, cores, high, low = sizes[GM], sizes["k"], sizes["yh"], sizes["yl"]
    n1, n2 = sizes[S1], sizes[S2]
    cols = high * low
    order = (GM, "k", "yh", "yl")
    turns = [[], []]
    for m in range(gm):
        for k in range(cores):
            for y in range(cols):
                to_m, half = y % gm, y // gm
                to_y = (to_m ^ m) * low + k
                for t in range(2):
                    to = (to_m * cores + (half ^ t)) * cols + to_y
                    turns[t].append(((m * cores + k) * cols + y, to))
    swap = [(0, 1), (1, 0)]
    up = [(y, (y + 1) % cols) for y in range(cols)]
    down = [(y, (y - 1) % cols) for y in range(cols)]

    def column():
        return lax.axis_index("yh") * low + lax.axis_index("yl")

    def local(three_index, vir_coef, owner_count, pair_index, occ_energy, vir_energy):
        width = vir_coef.shape[1]
        core, group, side = lax.axis_index("k"), lax.axis_index(GM), lax.axis_index("yl")
        rows = jnp.transpose(three_index, (1, 0, 2))
        turn_a, turn_b, kept, given, energy = transform(
            rows, vir_coef, owner_count, pair_index, occ_energy,
            lambda: (column() // gm, lax.axis_index("k")),
        )
        turned = [lax.ppermute(turn_a, order, turns[0]), lax.ppermute(turn_b, order, turns[1])]

        piece = width // (n1 * n2)
        offset = lax.axis_index(S1) * (width // n1) + lax.axis_index(S2) * piece
        first_vir = jnp.stack(
            [
                lax.dynamic_slice_in_dim(vir_energy, (h * gm + group) * width + offset, piece)
                for h in (core, 1 - core)
            ]
        )
        second_vir = lax.dynamic_slice_in_dim(vir_energy, column() * width, width)
        denominator = energy[0] - first_vir[:, :, None] - second_vir
        targets = group ^ jnp.arange(gm, dtype=jnp.int32)
        flip = (side ^ core).astype(jnp.int32).reshape(1)
        second = jnp.stack([kept, lax.ppermute(given, "k", swap)])
        turned, second, denominator, targets, flip = lax.optimization_barrier(
            (turned, second, denominator, targets, flip)
        )

        near = exchange(copied(turned, high), "yh")
        others = [lax.ppermute(second, GM, [(m, m ^ d) for m in range(gm)]) for d in (2, 1, 3)]
        near, others = lax.optimization_barrier((near, others))
        second_all = [second, others[1], others[0], others[2]]
        middle = high // 2
        far_low = lax.ppermute(near[:middle], ("yh", "yl"), up)
        far_high = lax.ppermute(near[middle:], ("yh", "yl"), down)
        first_all = [near, far_low, far_high]

        parts = coulomb_parts(flip, first_all, second_all, n1, n2)
        mine = added(exchange(parts, S1)).astype(bf16)
        share = added(exchange(mine, S2))
        amp = (share / denominator).astype(bf16)
        amp_all = spread(spread(amp, S2), S1)
        dens = exchange(density_parts(flip, targets, first_all, amp_all), GM)
        given = added(dens[:, 1])
        return finish(core, dens, lax.ppermute(given, "k", swap))

    return local


def solution(mesh):
    aux, row, col = (mesh.shape[name] for name in ("aux", "row", "col"))
    sizes = {"zl": 4, "zh": aux // 4, "k": 2, "x": row // 2, "yh": col // 2, "yl": 2}
    fine = Mesh(mesh.devices.reshape([sizes[name] for name in NAMES]), NAMES)
    owners = ("zh", "zl", "x", "k")
    return jax.shard_map(
        make_local(sizes),
        mesh=fine,
        in_specs=(P(owners, None, None), P(None, ("yh", "yl")), P(owners), P(), P(), P()),
        out_specs=P(owners, None, ("yh", "yl")),
        check_vma=False,
    )
```

```python
import jax
import jax.numpy as jnp
from jax import lax
from jax.experimental import pallas as pl
from jax.experimental.pallas import tpu as pltpu
from jax.sharding import Mesh, PartitionSpec as P

VMEM_LIMIT = 48 * 1024 * 1024
WIDE_LIMIT = 63 * 1024 * 1024
f32, bf16 = jnp.float32, jnp.bfloat16

NAMES = ("zh", "zl", "x", "k", "yh", "yl")
S1, S2 = "x", "zh"
GM = "zl"


def params():
    return pltpu.CompilerParams(vmem_limit_bytes=VMEM_LIMIT)


def transform(rows, coef, count, pairs, energies, place_of):
    occ, slots, basis = rows.shape
    width = coef.shape[1]
    step = 512
    steps = basis // step

    def kernel(
        count_hbm, pairs_hbm, energies_hbm, rows_hbm, coef_hbm,
        turn_a, turn_b, kept, given, energy,
        count_ref, pairs_ref, energies_ref, parts, coefs, held, sems, small,
    ):
        scalars = [
            pltpu.make_async_copy(count_hbm, count_ref, small.at[0]),
            pltpu.make_async_copy(pairs_hbm, pairs_ref, small.at[1]),
            pltpu.make_async_copy(energies_hbm, energies_ref, small.at[2]),
        ]
        copies = []
        for k in range(steps):
            span = pl.ds(k * step, step)
            copies.append(
                (
                    pltpu.make_async_copy(rows_hbm.at[:, :, span], parts.at[k], sems.at[0, k]),
                    pltpu.make_async_copy(coef_hbm.at[span], coefs.at[k], sems.at[1, k]),
                )
            )
        for pair in copies:
            for copy in pair:
                copy.start()
        for copy in scalars:
            copy.start()
        total = jnp.zeros((occ * slots, width), f32)
        for k in range(steps):
            for copy in copies[k]:
                copy.wait()
            part = parts[k].reshape(occ * slots, step)
            total += jnp.dot(part, coefs[k], preferred_element_type=f32)
        for copy in scalars:
            copy.wait()
        value = total.reshape(occ, slots, width)
        place = lax.broadcasted_iota(jnp.int32, (occ, slots, width), 1)
        held[...] = jnp.where(place < count_ref[0], value, 0.0).astype(bf16)
        half, core = place_of()
        turn_a[...] = held[pairs_ref[half, 0]]
        turn_b[...] = held[pairs_ref[1 - half, 0]]
        kept[...] = held[pairs_ref[core, 1]]
        given[...] = held[pairs_ref[1 - core, 1]]
        energy[0] = energies_ref[pairs_ref[core, 0]] + energies_ref[pairs_ref[core, 1]]

    out = jax.ShapeDtypeStruct((slots, width), bf16)
    hbm = pl.BlockSpec(memory_space=pl.ANY)
    vmem = pl.BlockSpec(memory_space=pltpu.VMEM)
    return pl.pallas_call(
        kernel,
        in_specs=[hbm] * 5,
        out_specs=[vmem] * 4 + [pl.BlockSpec(memory_space=pltpu.SMEM)],
        out_shape=[out] * 4 + [jax.ShapeDtypeStruct((1,), f32)],
        scratch_shapes=[
            pltpu.SMEM(count.shape, jnp.int32),
            pltpu.SMEM(pairs.shape, jnp.int32),
            pltpu.SMEM(energies.shape, f32),
            pltpu.VMEM((steps, occ, slots, step), bf16),
            pltpu.VMEM((steps, step, width), bf16),
            pltpu.VMEM((occ, slots, width), bf16),
            pltpu.SemaphoreType.DMA((2, steps)),
            pltpu.SemaphoreType.DMA((3,)),
        ],
        compiler_params=pltpu.CompilerParams(vmem_limit_bytes=WIDE_LIMIT),
    )(count, pairs, energies, rows, coef)


def flat(ref):
    return ref[...].reshape(-1, ref.shape[-1])


def coulomb_parts(side, first, second, n1, n2):
    groups, halves, slots, width = first[0].shape
    piece = width // (n1 * n2)

    def kernel(side_ref, near, low, high, *refs):
        out_ref = refs[-1]
        value = jnp.zeros((width, width), f32)
        held = [flat(near), jnp.concatenate([flat(low), flat(high)], axis=0)]
        for k in range(2):
            at = side_ref[0] if k == 0 else 1 - side_ref[0]
            b = jnp.concatenate([r[at] for r in refs[:-1]], axis=0)
            value += lax.dot_general(
                held[k], b, (((0,), (0,)), ((), ())), preferred_element_type=f32
            )
        out_ref[...] = value.astype(bf16).reshape(n1, n2, 1, piece, width)

    return pl.pallas_call(
        kernel,
        grid=(halves,),
        in_specs=[pl.BlockSpec(memory_space=pltpu.SMEM)]
        + [pl.BlockSpec((f.shape[0], 1, slots, width), lambda h: (0, h, 0, 0)) for f in first]
        + [pl.BlockSpec(r.shape, lambda h: (0, 0, 0)) for r in second],
        out_specs=pl.BlockSpec((n1, n2, 1, piece, width), lambda h: (0, 0, h, 0, 0)),
        out_shape=jax.ShapeDtypeStruct((n1, n2, halves, piece, width), bf16),
        compiler_params=params(),
    )(side, *first, *second)


def density_parts(side, targets, first, amplitude):
    groups, halves, slots, width = first[0].shape
    n1, n2, _, piece, _ = amplitude.shape

    def kernel(side_ref, targets_ref, near, low, high, amp_ref, out_ref):
        amps = [amp_ref[:, :, h].reshape(n1 * n2 * piece, width) for h in range(halves)]
        for k, refs in enumerate(((near,), (low, high))):
            value = 0.0
            for h in range(halves):
                a = jnp.concatenate([r[:, h].reshape(-1, width) for r in refs], axis=0)
                value += jnp.dot(a, amps[h], preferred_element_type=f32)
            value = value.astype(bf16).reshape(groups, slots, width)
            at = side_ref[0] if k == 0 else 1 - side_ref[0]
            for m in range(groups):
                out_ref[targets_ref[m], at] = value[m]

    smem = pl.BlockSpec(memory_space=pltpu.SMEM)
    vmem = pl.BlockSpec(memory_space=pltpu.VMEM)
    return pl.pallas_call(
        kernel,
        in_specs=[smem, smem] + [vmem] * 4,
        out_specs=vmem,
        out_shape=jax.ShapeDtypeStruct((groups, 2, slots, width), bf16),
        compiler_params=params(),
    )(side, targets, *first, amplitude)


def added(parts):
    total = parts[0].astype(f32)
    for k in range(1, parts.shape[0]):
        total = total + parts[k].astype(f32)
    return total


def finish(core, parts, came):
    groups, members, slots, width = parts.shape

    def kernel(core_ref, parts_ref, came_ref, out_ref):
        total = parts_ref[0, 0].astype(f32)
        for m in range(1, groups):
            total += parts_ref[m, 0].astype(f32)
        came = came_ref[...]
        own = core_ref[0] == 0
        out_ref[:, 0, :] = jnp.where(own, total, came)
        out_ref[:, 1, :] = jnp.where(own, came, total)

    vmem = pl.BlockSpec(memory_space=pltpu.VMEM)
    return pl.pallas_call(
        kernel,
        grid=(1,),
        in_specs=[
            pl.BlockSpec(memory_space=pltpu.SMEM),
            pl.BlockSpec((groups, 1, slots, width), lambda i: (0, 0, 0, 0)),
            pl.BlockSpec((slots, width), lambda i: (0, 0)),
        ],
        out_specs=pl.BlockSpec((slots, 2, width), lambda i: (0, 0, 0)),
        out_shape=jax.ShapeDtypeStruct((slots, 2, width), f32),
        compiler_params=params(),
    )(core.astype(jnp.int32).reshape(1), parts, came)


def exchange(parts, axis):
    return lax.all_to_all(parts, axis, 0, 0, tiled=True)


def copied(parts, count):
    def kernel(*refs):
        for n in range(count):
            for i, part in enumerate(refs[:-1]):
                refs[-1][n, i] = part[...]

    vmem = pl.BlockSpec(memory_space=pltpu.VMEM)
    shape = (count, len(parts)) + parts[0].shape
    return pl.pallas_call(
        kernel,
        in_specs=[vmem] * len(parts),
        out_specs=vmem,
        out_shape=jax.ShapeDtypeStruct(shape, parts[0].dtype),
        compiler_params=params(),
    )(*parts)


def spread(part, axis):
    copies = jnp.broadcast_to(part[None], (lax.axis_size(axis),) + part.shape)
    return exchange(lax.optimization_barrier(copies), axis)


def make_local(sizes):
    gm, cores, high, low = sizes[GM], sizes["k"], sizes["yh"], sizes["yl"]
    n1, n2 = sizes[S1], sizes[S2]
    cols = high * low
    order = (GM, "k", "yh", "yl")
    turns = [[], []]
    for m in range(gm):
        for k in range(cores):
            for y in range(cols):
                to_m, half = y % gm, y // gm
                to_y = (to_m ^ m) * low + k
                for t in range(2):
                    to = (to_m * cores + (half ^ t)) * cols + to_y
                    turns[t].append(((m * cores + k) * cols + y, to))
    swap = [(0, 1), (1, 0)]
    up = [(y, (y + 1) % cols) for y in range(cols)]
    down = [(y, (y - 1) % cols) for y in range(cols)]

    def column():
        return lax.axis_index("yh") * low + lax.axis_index("yl")

    def local(three_index, vir_coef, owner_count, pair_index, occ_energy, vir_energy):
        width = vir_coef.shape[1]
        core, group, side = lax.axis_index("k"), lax.axis_index(GM), lax.axis_index("yl")
        rows = jnp.transpose(three_index, (1, 0, 2))
        turn_a, turn_b, kept, given, energy = transform(
            rows, vir_coef, owner_count, pair_index, occ_energy,
            lambda: (column() // gm, lax.axis_index("k")),
        )
        turned = [lax.ppermute(turn_a, order, turns[0]), lax.ppermute(turn_b, order, turns[1])]

        piece = width // (n1 * n2)
        offset = lax.axis_index(S1) * (width // n1) + lax.axis_index(S2) * piece
        first_vir = jnp.stack(
            [
                lax.dynamic_slice_in_dim(vir_energy, (h * gm + group) * width + offset, piece)
                for h in (core, 1 - core)
            ]
        )
        second_vir = lax.dynamic_slice_in_dim(vir_energy, column() * width, width)
        denominator = energy[0] - first_vir[:, :, None] - second_vir
        targets = group ^ jnp.arange(gm, dtype=jnp.int32)
        flip = (side ^ core).astype(jnp.int32).reshape(1)
        second = jnp.stack([kept, lax.ppermute(given, "k", swap)])
        turned, second, denominator, targets, flip = lax.optimization_barrier(
            (turned, second, denominator, targets, flip)
        )

        near = lax.all_gather(copied(turned, 1)[0], "yh", axis=0, tiled=False)
        others = [lax.ppermute(second, GM, [(m, m ^ d) for m in range(gm)]) for d in (2, 1, 3)]
        near, others = lax.optimization_barrier((near, others))
        second_all = [second, others[1], others[0], others[2]]
        middle = high // 2
        far_low = lax.ppermute(near[:middle], ("yh", "yl"), up)
        far_high = lax.ppermute(near[middle:], ("yh", "yl"), down)
        first_all = [near, far_low, far_high]

        parts = coulomb_parts(flip, first_all, second_all, n1, n2)
        mine = added(exchange(parts, S1)).astype(bf16)
        share = added(exchange(mine, S2))
        amp = (share / denominator).astype(bf16)
        amp_all = spread(spread(amp, S2), S1)
        dens = exchange(density_parts(flip, targets, first_all, amp_all), GM)
        given = added(dens[:, 1])
        return finish(core, dens, lax.ppermute(given, "k", swap))

    return local


def solution(mesh):
    aux, row, col = (mesh.shape[name] for name in ("aux", "row", "col"))
    sizes = {"zl": 4, "zh": aux // 4, "k": 2, "x": row // 2, "yh": col // 2, "yl": 2}
    fine = Mesh(mesh.devices.reshape([sizes[name] for name in NAMES]), NAMES)
    owners = ("zh", "zl", "x", "k")
    return jax.shard_map(
        make_local(sizes),
        mesh=fine,
        in_specs=(P(owners, None, None), P(None, ("yh", "yl")), P(owners), P(), P(), P()),
        out_specs=P(owners, None, ("yh", "yl")),
        check_vma=False,
    )
```

```python
import jax
import jax.numpy as jnp
from jax import lax
from jax.experimental import pallas as pl
from jax.experimental.pallas import tpu as pltpu
from jax.sharding import Mesh, PartitionSpec as P

VMEM_LIMIT = 48 * 1024 * 1024
WIDE_LIMIT = 63 * 1024 * 1024
f32, bf16 = jnp.float32, jnp.bfloat16

NAMES = ("zh", "zl", "x", "k", "yh", "yl")
S1, S2 = "x", "zh"
GM = "zl"


def params():
    return pltpu.CompilerParams(vmem_limit_bytes=VMEM_LIMIT)


def transform(rows, coef, count, pairs, energies, place_of):
    occ, slots, basis = rows.shape
    width = coef.shape[1]
    step = 512
    steps = basis // step

    def kernel(
        count_hbm, pairs_hbm, energies_hbm, rows_hbm, coef_hbm,
        turn_a, turn_b, kept, given, energy,
        count_ref, pairs_ref, energies_ref, parts, coefs, held, sems, small,
    ):
        scalars = [
            pltpu.make_async_copy(count_hbm, count_ref, small.at[0]),
            pltpu.make_async_copy(pairs_hbm, pairs_ref, small.at[1]),
            pltpu.make_async_copy(energies_hbm, energies_ref, small.at[2]),
        ]
        copies = []
        for k in range(steps):
            span = pl.ds(k * step, step)
            copies.append(
                (
                    pltpu.make_async_copy(rows_hbm.at[:, :, span], parts.at[k], sems.at[0, k]),
                    pltpu.make_async_copy(coef_hbm.at[span], coefs.at[k], sems.at[1, k]),
                )
            )
        for pair in copies:
            for copy in pair:
                copy.start()
        for copy in scalars:
            copy.start()
        total = jnp.zeros((occ * slots, width), f32)
        for k in range(steps):
            for copy in copies[k]:
                copy.wait()
            part = parts[k].reshape(occ * slots, step)
            total += jnp.dot(part, coefs[k], preferred_element_type=f32)
        for copy in scalars:
            copy.wait()
        value = total.reshape(occ, slots, width)
        place = lax.broadcasted_iota(jnp.int32, (occ, slots, width), 1)
        held[...] = jnp.where(place < count_ref[0], value, 0.0).astype(bf16)
        half, core = place_of()
        turn_a[...] = held[pairs_ref[half, 0]]
        turn_b[...] = held[pairs_ref[1 - half, 0]]
        kept[...] = held[pairs_ref[core, 1]]
        given[...] = held[pairs_ref[1 - core, 1]]
        energy[0] = energies_ref[pairs_ref[core, 0]] + energies_ref[pairs_ref[core, 1]]

    out = jax.ShapeDtypeStruct((slots, width), bf16)
    hbm = pl.BlockSpec(memory_space=pl.ANY)
    vmem = pl.BlockSpec(memory_space=pltpu.VMEM)
    return pl.pallas_call(
        kernel,
        in_specs=[hbm] * 5,
        out_specs=[vmem] * 4 + [pl.BlockSpec(memory_space=pltpu.SMEM)],
        out_shape=[out] * 4 + [jax.ShapeDtypeStruct((1,), f32)],
        scratch_shapes=[
            pltpu.SMEM(count.shape, jnp.int32),
            pltpu.SMEM(pairs.shape, jnp.int32),
            pltpu.SMEM(energies.shape, f32),
            pltpu.VMEM((steps, occ, slots, step), bf16),
            pltpu.VMEM((steps, step, width), bf16),
            pltpu.VMEM((occ, slots, width), bf16),
            pltpu.SemaphoreType.DMA((2, steps)),
            pltpu.SemaphoreType.DMA((3,)),
        ],
        compiler_params=pltpu.CompilerParams(vmem_limit_bytes=WIDE_LIMIT),
    )(count, pairs, energies, rows, coef)


def flat(ref):
    return ref[...].reshape(-1, ref.shape[-1])


def coulomb_parts(side, first, second, n1, n2):
    groups, halves, slots, width = first[0].shape
    piece = width // (n1 * n2)

    def kernel(side_ref, near, low, high, *refs):
        out_ref = refs[-1]
        value = jnp.zeros((width, width), f32)
        held = [flat(near), jnp.concatenate([flat(low), flat(high)], axis=0)]
        for k in range(2):
            at = side_ref[0] if k == 0 else 1 - side_ref[0]
            own, across, beside = refs[:-1]
            b = jnp.concatenate([own[at], beside[0, at], across[at], beside[1, at]], axis=0)
            value += lax.dot_general(
                held[k], b, (((0,), (0,)), ((), ())), preferred_element_type=f32
            )
        out_ref[...] = value.astype(bf16).reshape(n1, n2, 1, piece, width)

    return pl.pallas_call(
        kernel,
        grid=(halves,),
        in_specs=[pl.BlockSpec(memory_space=pltpu.SMEM)]
        + [pl.BlockSpec((f.shape[0], 1, slots, width), lambda h: (0, h, 0, 0)) for f in first]
        + [pl.BlockSpec(r.shape, lambda h, n=r.ndim: (0,) * n) for r in second],
        out_specs=pl.BlockSpec((n1, n2, 1, piece, width), lambda h: (0, 0, h, 0, 0)),
        out_shape=jax.ShapeDtypeStruct((n1, n2, halves, piece, width), bf16),
        compiler_params=params(),
    )(side, *first, *second)


def density_parts(side, targets, first, amplitude):
    groups, halves, slots, width = first[0].shape
    n1, n2, _, piece, _ = amplitude.shape

    def kernel(side_ref, targets_ref, near, low, high, amp_ref, out_ref):
        amps = [amp_ref[:, :, h].reshape(n1 * n2 * piece, width) for h in range(halves)]
        for k, refs in enumerate(((near,), (low, high))):
            value = 0.0
            for h in range(halves):
                a = jnp.concatenate([r[:, h].reshape(-1, width) for r in refs], axis=0)
                value += jnp.dot(a, amps[h], preferred_element_type=f32)
            value = value.astype(bf16).reshape(groups, slots, width)
            at = side_ref[0] if k == 0 else 1 - side_ref[0]
            for m in range(groups):
                out_ref[targets_ref[m], at] = value[m]

    smem = pl.BlockSpec(memory_space=pltpu.SMEM)
    vmem = pl.BlockSpec(memory_space=pltpu.VMEM)
    return pl.pallas_call(
        kernel,
        in_specs=[smem, smem] + [vmem] * 4,
        out_specs=vmem,
        out_shape=jax.ShapeDtypeStruct((groups, 2, slots, width), bf16),
        compiler_params=params(),
    )(side, targets, *first, amplitude)


def added(parts):
    total = parts[0].astype(f32)
    for k in range(1, parts.shape[0]):
        total = total + parts[k].astype(f32)
    return total


def finish(core, parts, came):
    groups, members, slots, width = parts.shape

    def kernel(core_ref, parts_ref, came_ref, out_ref):
        total = parts_ref[0, 0].astype(f32)
        for m in range(1, groups):
            total += parts_ref[m, 0].astype(f32)
        came = came_ref[...]
        own = core_ref[0] == 0
        out_ref[:, 0, :] = jnp.where(own, total, came)
        out_ref[:, 1, :] = jnp.where(own, came, total)

    vmem = pl.BlockSpec(memory_space=pltpu.VMEM)
    return pl.pallas_call(
        kernel,
        grid=(1,),
        in_specs=[
            pl.BlockSpec(memory_space=pltpu.SMEM),
            pl.BlockSpec((groups, 1, slots, width), lambda i: (0, 0, 0, 0)),
            pl.BlockSpec((slots, width), lambda i: (0, 0)),
        ],
        out_specs=pl.BlockSpec((slots, 2, width), lambda i: (0, 0, 0)),
        out_shape=jax.ShapeDtypeStruct((slots, 2, width), f32),
        compiler_params=params(),
    )(core.astype(jnp.int32).reshape(1), parts, came)


def exchange(parts, axis):
    return lax.all_to_all(parts, axis, 0, 0, tiled=True)


def copied(parts, count):
    def kernel(*refs):
        for n in range(count):
            for i, part in enumerate(refs[:-1]):
                refs[-1][n, i] = part[...]

    vmem = pl.BlockSpec(memory_space=pltpu.VMEM)
    shape = (count, len(parts)) + parts[0].shape
    return pl.pallas_call(
        kernel,
        in_specs=[vmem] * len(parts),
        out_specs=vmem,
        out_shape=jax.ShapeDtypeStruct(shape, parts[0].dtype),
        compiler_params=params(),
    )(*parts)


def spread(part, axis):
    copies = jnp.broadcast_to(part[None], (lax.axis_size(axis),) + part.shape)
    return exchange(lax.optimization_barrier(copies), axis)


def make_local(sizes):
    gm, cores, high, low = sizes[GM], sizes["k"], sizes["yh"], sizes["yl"]
    n1, n2 = sizes[S1], sizes[S2]
    cols = high * low
    order = (GM, "k", "yh", "yl")
    turns = [[], []]
    for m in range(gm):
        for k in range(cores):
            for y in range(cols):
                to_m, half = y % gm, y // gm
                to_y = (to_m ^ m) * low + k
                for t in range(2):
                    to = (to_m * cores + (half ^ t)) * cols + to_y
                    turns[t].append(((m * cores + k) * cols + y, to))
    swap = [(0, 1), (1, 0)]
    up = [(y, (y + 1) % cols) for y in range(cols)]
    down = [(y, (y - 1) % cols) for y in range(cols)]

    def column():
        return lax.axis_index("yh") * low + lax.axis_index("yl")

    def local(three_index, vir_coef, owner_count, pair_index, occ_energy, vir_energy):
        width = vir_coef.shape[1]
        core, group, side = lax.axis_index("k"), lax.axis_index(GM), lax.axis_index("yl")
        rows = jnp.transpose(three_index, (1, 0, 2))
        turn_a, turn_b, kept, given, energy = transform(
            rows, vir_coef, owner_count, pair_index, occ_energy,
            lambda: (column() // gm, lax.axis_index("k")),
        )
        turned = [lax.ppermute(turn_a, order, turns[0]), lax.ppermute(turn_b, order, turns[1])]

        piece = width // (n1 * n2)
        offset = lax.axis_index(S1) * (width // n1) + lax.axis_index(S2) * piece
        first_vir = jnp.stack(
            [
                lax.dynamic_slice_in_dim(vir_energy, (h * gm + group) * width + offset, piece)
                for h in (core, 1 - core)
            ]
        )
        second_vir = lax.dynamic_slice_in_dim(vir_energy, column() * width, width)
        denominator = energy[0] - first_vir[:, :, None] - second_vir
        targets = group ^ jnp.arange(gm, dtype=jnp.int32)
        flip = (side ^ core).astype(jnp.int32).reshape(1)
        second = jnp.stack([kept, lax.ppermute(given, "k", swap)])
        turned, second, denominator, targets, flip = lax.optimization_barrier(
            (turned, second, denominator, targets, flip)
        )

        near = lax.all_gather(copied(turned, 1)[0], "yh", axis=0, tiled=False)
        across = lax.ppermute(second, GM, [(m, m ^ 2) for m in range(gm)])
        near, across = lax.optimization_barrier((near, across))
        held = jnp.stack([second, across])
        beside = lax.ppermute(held, GM, [(m, m ^ 1) for m in range(gm)])
        second_all = [second, across, beside]
        middle = high // 2
        far_low = lax.ppermute(near[:middle], ("yh", "yl"), up)
        far_high = lax.ppermute(near[middle:], ("yh", "yl"), down)
        first_all = [near, far_low, far_high]

        parts = coulomb_parts(flip, first_all, second_all, n1, n2)
        mine = added(exchange(parts, S1)).astype(bf16)
        share = added(exchange(mine, S2))
        amp = (share / denominator).astype(bf16)
        amp_all = spread(spread(amp, S2), S1)
        dens = exchange(density_parts(flip, targets, first_all, amp_all), GM)
        given = added(dens[:, 1])
        return finish(core, dens, lax.ppermute(given, "k", swap))

    return local


def solution(mesh):
    aux, row, col = (mesh.shape[name] for name in ("aux", "row", "col"))
    sizes = {"zl": 4, "zh": aux // 4, "k": 2, "x": row // 2, "yh": col // 2, "yl": 2}
    fine = Mesh(mesh.devices.reshape([sizes[name] for name in NAMES]), NAMES)
    owners = ("zh", "zl", "x", "k")
    return jax.shard_map(
        make_local(sizes),
        mesh=fine,
        in_specs=(P(owners, None, None), P(None, ("yh", "yl")), P(owners), P(), P(), P()),
        out_specs=P(owners, None, ("yh", "yl")),
        check_vma=False,
    )
```

```python
import jax
import jax.numpy as jnp
from jax import lax
from jax.experimental import pallas as pl
from jax.experimental.pallas import tpu as pltpu
from jax.sharding import Mesh, PartitionSpec as P

VMEM_LIMIT = 48 * 1024 * 1024
WIDE_LIMIT = 63 * 1024 * 1024
f32, bf16 = jnp.float32, jnp.bfloat16

NAMES = ("zh", "zl", "x", "k", "yh", "yl")
S1, S2 = "x", "zh"
GM = "zl"


def params():
    return pltpu.CompilerParams(vmem_limit_bytes=VMEM_LIMIT)


def transform(rows, coef, count, pairs, energies, place_of):
    occ, slots, basis = rows.shape
    width = coef.shape[1]
    step = 512
    steps = basis // step

    def kernel(
        count_hbm, pairs_hbm, energies_hbm, rows_hbm, coef_hbm,
        turn_a, turn_b, kept, given, energy,
        count_ref, pairs_ref, energies_ref, parts, coefs, held, sems, small,
    ):
        scalars = [
            pltpu.make_async_copy(count_hbm, count_ref, small.at[0]),
            pltpu.make_async_copy(pairs_hbm, pairs_ref, small.at[1]),
            pltpu.make_async_copy(energies_hbm, energies_ref, small.at[2]),
        ]
        copies = []
        for k in range(steps):
            span = pl.ds(k * step, step)
            copies.append(
                (
                    pltpu.make_async_copy(rows_hbm.at[:, :, span], parts.at[k], sems.at[0, k]),
                    pltpu.make_async_copy(coef_hbm.at[span], coefs.at[k], sems.at[1, k]),
                )
            )
        for pair in copies:
            for copy in pair:
                copy.start()
        for copy in scalars:
            copy.start()
        total = jnp.zeros((occ * slots, width), f32)
        for k in range(steps):
            for copy in copies[k]:
                copy.wait()
            part = parts[k].reshape(occ * slots, step)
            total += jnp.dot(part, coefs[k], preferred_element_type=f32)
        for copy in scalars:
            copy.wait()
        value = total.reshape(occ, slots, width)
        place = lax.broadcasted_iota(jnp.int32, (occ, slots, width), 1)
        held[...] = jnp.where(place < count_ref[0], value, 0.0).astype(bf16)
        half, core = place_of()
        turn_a[...] = held[pairs_ref[half, 0]]
        turn_b[...] = held[pairs_ref[1 - half, 0]]
        kept[...] = held[pairs_ref[core, 1]]
        given[...] = held[pairs_ref[1 - core, 1]]
        energy[0] = energies_ref[pairs_ref[core, 0]] + energies_ref[pairs_ref[core, 1]]

    out = jax.ShapeDtypeStruct((slots, width), bf16)
    hbm = pl.BlockSpec(memory_space=pl.ANY)
    vmem = pl.BlockSpec(memory_space=pltpu.VMEM)
    return pl.pallas_call(
        kernel,
        in_specs=[hbm] * 5,
        out_specs=[vmem] * 4 + [pl.BlockSpec(memory_space=pltpu.SMEM)],
        out_shape=[out] * 4 + [jax.ShapeDtypeStruct((1,), f32)],
        scratch_shapes=[
            pltpu.SMEM(count.shape, jnp.int32),
            pltpu.SMEM(pairs.shape, jnp.int32),
            pltpu.SMEM(energies.shape, f32),
            pltpu.VMEM((steps, occ, slots, step), bf16),
            pltpu.VMEM((steps, step, width), bf16),
            pltpu.VMEM((occ, slots, width), bf16),
            pltpu.SemaphoreType.DMA((2, steps)),
            pltpu.SemaphoreType.DMA((3,)),
        ],
        compiler_params=pltpu.CompilerParams(vmem_limit_bytes=WIDE_LIMIT),
    )(count, pairs, energies, rows, coef)


def flat(ref):
    return ref[...].reshape(-1, ref.shape[-1])


def coulomb_parts(side, first, second, n1, n2):
    groups, halves, slots, width = first[0].shape
    piece = width // (n1 * n2)

    def kernel(side_ref, near, low, high, *refs):
        out_ref = refs[-1]
        value = jnp.zeros((width, width), f32)
        held = [flat(near), jnp.concatenate([flat(low), flat(high)], axis=0)]
        for k in range(2):
            at = side_ref[0] if k == 0 else 1 - side_ref[0]
            own, across, beside = refs[:-1]
            b = jnp.concatenate([own[at], beside[0, at], across[at], beside[1, at]], axis=0)
            value += lax.dot_general(
                held[k], b, (((0,), (0,)), ((), ())), preferred_element_type=f32
            )
        out_ref[...] = value.astype(bf16).reshape(n1, n2, 1, piece, width)

    return pl.pallas_call(
        kernel,
        grid=(halves,),
        in_specs=[pl.BlockSpec(memory_space=pltpu.SMEM)]
        + [pl.BlockSpec((f.shape[0], 1, slots, width), lambda h: (0, h, 0, 0)) for f in first]
        + [pl.BlockSpec(r.shape, lambda h, n=r.ndim: (0,) * n) for r in second],
        out_specs=pl.BlockSpec((n1, n2, 1, piece, width), lambda h: (0, 0, h, 0, 0)),
        out_shape=jax.ShapeDtypeStruct((n1, n2, halves, piece, width), bf16),
        compiler_params=params(),
    )(side, *first, *second)


def density_parts(side, targets, first, amplitude):
    groups, halves, slots, width = first[0].shape
    n1, n2, _, piece, _ = amplitude.shape

    def kernel(side_ref, targets_ref, near, low, high, amp_ref, out_ref):
        amps = [amp_ref[:, :, h].reshape(n1 * n2 * piece, width) for h in range(halves)]
        for k, refs in enumerate(((near,), (low, high))):
            value = 0.0
            for h in range(halves):
                a = jnp.concatenate([r[:, h].reshape(-1, width) for r in refs], axis=0)
                value += jnp.dot(a, amps[h], preferred_element_type=f32)
            value = value.astype(bf16).reshape(groups, slots, width)
            at = side_ref[0] if k == 0 else 1 - side_ref[0]
            for m in range(groups):
                out_ref[targets_ref[m], at] = value[m]

    smem = pl.BlockSpec(memory_space=pltpu.SMEM)
    vmem = pl.BlockSpec(memory_space=pltpu.VMEM)
    return pl.pallas_call(
        kernel,
        in_specs=[smem, smem] + [vmem] * 4,
        out_specs=vmem,
        out_shape=jax.ShapeDtypeStruct((groups, 2, slots, width), bf16),
        compiler_params=params(),
    )(side, targets, *first, amplitude)


def added(parts):
    total = parts[0].astype(f32)
    for k in range(1, parts.shape[0]):
        total = total + parts[k].astype(f32)
    return total


def finish(core, parts, came):
    groups, members, slots, width = parts.shape

    def kernel(core_ref, parts_ref, came_ref, out_ref):
        total = parts_ref[0, 0].astype(f32)
        for m in range(1, groups):
            total += parts_ref[m, 0].astype(f32)
        came = came_ref[...]
        own = core_ref[0] == 0
        out_ref[:, 0, :] = jnp.where(own, total, came)
        out_ref[:, 1, :] = jnp.where(own, came, total)

    vmem = pl.BlockSpec(memory_space=pltpu.VMEM)
    return pl.pallas_call(
        kernel,
        grid=(1,),
        in_specs=[
            pl.BlockSpec(memory_space=pltpu.SMEM),
            pl.BlockSpec((groups, 1, slots, width), lambda i: (0, 0, 0, 0)),
            pl.BlockSpec((slots, width), lambda i: (0, 0)),
        ],
        out_specs=pl.BlockSpec((slots, 2, width), lambda i: (0, 0, 0)),
        out_shape=jax.ShapeDtypeStruct((slots, 2, width), f32),
        compiler_params=params(),
    )(core.astype(jnp.int32).reshape(1), parts, came)


def exchange(parts, axis):
    return lax.all_to_all(parts, axis, 0, 0, tiled=True)


def copied(parts, more, count):
    shape = parts[0].shape

    def kernel(a, b, c, d, copies_ref, more_ref):
        for n in range(count):
            copies_ref[n, 0] = a[...]
            copies_ref[n, 1] = b[...]
        more_ref[0] = c[...]
        more_ref[1] = d[...]

    vmem = pl.BlockSpec(memory_space=pltpu.VMEM)
    return pl.pallas_call(
        kernel,
        in_specs=[vmem] * 4,
        out_specs=[vmem] * 2,
        out_shape=[
            jax.ShapeDtypeStruct((count, 2) + shape, bf16),
            jax.ShapeDtypeStruct((2,) + shape, bf16),
        ],
        compiler_params=params(),
    )(*parts, *more)


def spread(part, axis):
    copies = jnp.broadcast_to(part[None], (lax.axis_size(axis),) + part.shape)
    return exchange(lax.optimization_barrier(copies), axis)


def make_local(sizes):
    gm, cores, high, low = sizes[GM], sizes["k"], sizes["yh"], sizes["yl"]
    n1, n2 = sizes[S1], sizes[S2]
    cols = high * low
    order = (GM, "k", "yh", "yl")
    turns = [[], []]
    for m in range(gm):
        for k in range(cores):
            for y in range(cols):
                to_m, half = y % gm, y // gm
                to_y = (to_m ^ m) * low + k
                for t in range(2):
                    to = (to_m * cores + (half ^ t)) * cols + to_y
                    turns[t].append(((m * cores + k) * cols + y, to))
    swap = [(0, 1), (1, 0)]
    up = [(y, (y + 1) % cols) for y in range(cols)]
    down = [(y, (y - 1) % cols) for y in range(cols)]

    def column():
        return lax.axis_index("yh") * low + lax.axis_index("yl")

    def local(three_index, vir_coef, owner_count, pair_index, occ_energy, vir_energy):
        width = vir_coef.shape[1]
        core, group, side = lax.axis_index("k"), lax.axis_index(GM), lax.axis_index("yl")
        rows = jnp.transpose(three_index, (1, 0, 2))
        turn_a, turn_b, kept, given, energy = transform(
            rows, vir_coef, owner_count, pair_index, occ_energy,
            lambda: (column() // gm, lax.axis_index("k")),
        )
        turned = [lax.ppermute(turn_a, order, turns[0]), lax.ppermute(turn_b, order, turns[1])]

        piece = width // (n1 * n2)
        offset = lax.axis_index(S1) * (width // n1) + lax.axis_index(S2) * piece
        first_vir = jnp.stack(
            [
                lax.dynamic_slice_in_dim(vir_energy, (h * gm + group) * width + offset, piece)
                for h in (core, 1 - core)
            ]
        )
        second_vir = lax.dynamic_slice_in_dim(vir_energy, column() * width, width)
        denominator = energy[0] - first_vir[:, :, None] - second_vir
        targets = group ^ jnp.arange(gm, dtype=jnp.int32)
        flip = (side ^ core).astype(jnp.int32).reshape(1)
        copies, second = copied(turned, [kept, lax.ppermute(given, "k", swap)], 1)
        near = lax.all_gather(copies[0], "yh", axis=0, tiled=False)
        across = lax.ppermute(second, GM, [(m, m ^ 2) for m in range(gm)])
        near, across = lax.optimization_barrier((near, across))
        held = jnp.stack([second, across])
        beside = lax.ppermute(held, GM, [(m, m ^ 1) for m in range(gm)])
        second_all = [second, across, beside]
        middle = high // 2
        far_low = lax.ppermute(near[:middle], ("yh", "yl"), up)
        far_high = lax.ppermute(near[middle:], ("yh", "yl"), down)
        far_low, far_high, denominator, targets, flip = lax.optimization_barrier(
            (far_low, far_high, denominator, targets, flip)
        )
        first_all = [near, far_low, far_high]

        parts = coulomb_parts(flip, first_all, second_all, n1, n2)
        mine = added(exchange(parts, S1)).astype(bf16)
        share = added(exchange(mine, S2))
        amp = (share / denominator).astype(bf16)
        amp_all = spread(spread(amp, S2), S1)
        dens = exchange(density_parts(flip, targets, first_all, amp_all), GM)
        given = added(dens[:, 1])
        return finish(core, dens, lax.ppermute(given, "k", swap))

    return local


def solution(mesh):
    aux, row, col = (mesh.shape[name] for name in ("aux", "row", "col"))
    sizes = {"zl": 4, "zh": aux // 4, "k": 2, "x": row // 2, "yh": col // 2, "yl": 2}
    fine = Mesh(mesh.devices.reshape([sizes[name] for name in NAMES]), NAMES)
    owners = ("zh", "zl", "x", "k")
    return jax.shard_map(
        make_local(sizes),
        mesh=fine,
        in_specs=(P(owners, None, None), P(None, ("yh", "yl")), P(owners), P(), P(), P()),
        out_specs=P(owners, None, ("yh", "yl")),
        check_vma=False,
    )
```
